32 devices in a mesh: group: 2 (over y), dec: 16 (over z, x, core).
Axes of the slice: x: 2, y: 2, z: 4, core: 2. Of those that a mesh axis runs over, the one named last changes fastest.
Arguments:
- image_states: bfloat16 [56, 256, 8192], P('group', 'dec'), parts along dimension 0, may hold values from -6 to 6
- w_key: bfloat16 [8192, 512], P('dec'), may hold values from -0.0625 to 0.0625
- w_value: bfloat16 [8192, 512], P('dec'), may hold values from -0.25 to 0.25
- key_gain: float32 [128], replicated, may hold values from 0.5 to 2
- query_gain: float32 [128], replicated, may hold values from 0.5 to 2
- head_gate: float32 [32], replicated, may hold values from 0.3 to 2
- queries: bfloat16 [32, 256, 4096], P(('group', 'dec')), parts along dimension 0, may hold values from -6 to 6
- tile_counts: int32 [32], P('group'), parts along dimension 0, may hold values from 1 to 4, 28 in all
- owner_of: int32 [32], P('group'), parts along dimension 0, may hold values from 0 to 15, each once
Outputs:
- attended: bfloat16 [32, 256, 4096], P(('group', 'dec')), parts along dimension 0
The draws below stay inside these ranges and needn't reach their ends.
There are 2 independent parts, one for each index of `group`. The reference program is written for one: setup_inputs(seed, part) draws one part's arguments, and reference() takes and returns one part's arrays. A program takes and returns all parts, laid end to end along the dimension named above; an argument that names none is the same for every part. Nothing has to cross between parts.
Inputs may be any that keep to these rules, and one draw needn't show every extreme that they name: `tile_counts`: the counts sum to 28; some request has exactly 4 tiles. `owner_of`: every device index appears exactly once.
All inputs are finite; a program needn't handle non-finite values.
Results may differ from the reference program's by a relative error of at most 0.0087.
Values may be sent and summed in bfloat16 or wider, within the bound.
A program may use at most 128 MiB of HBM per device.

```python
import math
import jax
import jax.numpy as jnp
import numpy as np
from jax import lax

D = 8192
HEAD = 128
KV_HEADS = 4
QUERY_HEADS = 8
TEXT = 256
TILE_TOK = 256
MAX_TILES = 4
REQUESTS = 16
TILES = 28


def level_of(rng, shape, shards, least, high):
    factor_of = 1.0
    for dim, shards_of in shards:
        draws = jax.random.uniform(jax.random.fold_in(jax.random.fold_in(rng, 6), dim), (shards_of,), jnp.float32, least / len(shards), high / len(shards))
        factor_of = factor_of * jnp.repeat(jnp.exp(draws), shape[dim] // shards_of).reshape((-1,) + (1,) * (len(shape) - 1 - dim))
    return factor_of


def length_profile(amount, total, limit, slope):
    loads = [(1 << 20) // math.isqrt(rank ** slope) + 1 for rank in range(2, amount + 1)]
    rest, given = total - limit - (amount - 1), [1] * (amount - 1)
    while rest > 0:
        free = [i for i in range(amount - 1) if given[i] < limit]
        whole, remaining = sum([loads[i] for i in free]), rest
        for i in free:
            more = min(limit - given[i], max(1, remaining * loads[i] // whole), rest)
            given[i] = given[i] + more
            rest = rest - more
    return np.array([limit] + given)


def ragged(own_key, amount, total, bound, lean):
    if amount == 2:
        one = jax.random.randint(own_key, (), max(1, total - bound), min(bound, total - 1) + 1)
        return jnp.stack([one, total - one])
    lengths = jnp.asarray(length_profile(amount, total, bound, lean), jnp.int32)
    twos = (amount - 1) // 2
    source_of, taker = lengths[1:1 + 2 * twos:2], lengths[2:2 + 2 * twos:2]
    slack = jnp.minimum(source_of - 1, bound - taker)
    passed = jax.random.randint(jax.random.fold_in(own_key, 1), (twos,), 0, 1 << 20) % (slack + 1)
    lengths = lengths.at[1:1 + 2 * twos:2].set(source_of - passed).at[2:2 + 2 * twos:2].set(taker + passed)
    return lengths[jax.random.permutation(jax.random.fold_in(own_key, 2), amount)]


def bell_draw(stream_key, dims, width, most, shards=(), kind=jnp.bfloat16):
    drawn = jax.random.normal(stream_key, dims, jnp.float32) * width
    if len(shards) > 0:
        drawn = level_of(stream_key, dims, shards, -0.22, 0.18) * drawn
    return jnp.clip(drawn, min=-most, max=most).astype(kind)


def setup_inputs(seed: int = 0, part: int = 0) -> dict:
    seeds = jax.random.split(jax.random.key(seed), 10)
    part_splits = jax.random.split(jax.random.fold_in(seeds[9], part), 10)
    image_states = bell_draw(part_splits[0], (TILES, TILE_TOK, D), 1.0, 6.0, ((1, 16),))
    w_key = bell_draw(seeds[1], (D, KV_HEADS * HEAD), D ** -0.5, 0.0625, ((0, 16),))
    w_value = bell_draw(seeds[2], (D, KV_HEADS * HEAD), (D // 16) ** -0.5, 0.25, ((0, 16),))
    key_gain = jnp.clip(jax.random.uniform(seeds[3], (HEAD,), jnp.float32, 0.5, 2.0), 0.5, 2.0)
    query_gain = jnp.clip(jax.random.uniform(seeds[4], (HEAD,), jnp.float32, 0.5, 2.0), 0.5, 2.0)
    head_gate = jnp.clip(jax.random.uniform(seeds[5], (KV_HEADS * QUERY_HEADS,), jnp.float32, 0.3, 2.0), 0.3, 2.0)
    queries = bell_draw(part_splits[6], (REQUESTS, TEXT, KV_HEADS * QUERY_HEADS * HEAD), 1.0, 6.0, ((0, 16),))
    tile_counts = ragged(part_splits[7], REQUESTS, TILES, MAX_TILES, 2).astype(jnp.int32)
    owner_of = jax.random.permutation(part_splits[8], REQUESTS).astype(jnp.int32)
    return dict(image_states=image_states, w_key=w_key, w_value=w_value, key_gain=key_gain, query_gain=query_gain, head_gate=head_gate, queries=queries, tile_counts=tile_counts, owner_of=owner_of)


EPS = 1e-05

def rms_scale(values, gain):
    mean_square = lax.optimization_barrier(jnp.mean(values * values, axis=-1, keepdims=True))
    return values * lax.rsqrt(mean_square + EPS) * gain

def reference(image_states, w_key, w_value, key_gain, query_gain, head_gate, queries, tile_counts, owner_of):
    flat_rows = image_states.reshape(TILES * TILE_TOK, D)
    key_part = jnp.dot(flat_rows, w_key, preferred_element_type=jnp.float32).reshape(TILES * TILE_TOK, KV_HEADS, HEAD)
    key_all = rms_scale(key_part, key_gain).astype(jnp.bfloat16).reshape(TILES, TILE_TOK, KV_HEADS, HEAD)
    value_all = jnp.dot(flat_rows, w_value, preferred_element_type=jnp.float32).astype(jnp.bfloat16).reshape(TILES, TILE_TOK, KV_HEADS, HEAD)
    request_ids = jnp.arange(REQUESTS, dtype=jnp.int32)
    counts = tile_counts.astype(jnp.int32)
    starts = (jnp.cumsum(counts) - counts).astype(jnp.int32)
    slot_ids = jnp.arange(MAX_TILES, dtype=jnp.int32)
    gate_value = jnp.tanh(head_gate).reshape(KV_HEADS, QUERY_HEADS)

    def one_owner(item):
        device_id, query_block = item
        request = jnp.sum(jnp.where(owner_of == device_id, request_ids, 0)).astype(jnp.int32)
        first = jnp.sum(jnp.where(request_ids == request, starts, 0)).astype(jnp.int32)
        count = jnp.sum(jnp.where(request_ids == request, counts, 0)).astype(jnp.int32)
        wanted = jnp.minimum(first + slot_ids, TILES - 1).astype(jnp.int32)
        key_list = jnp.take(key_all, wanted, axis=0).reshape(MAX_TILES * TILE_TOK, KV_HEADS, HEAD)
        value_list = jnp.take(value_all, wanted, axis=0).reshape(MAX_TILES * TILE_TOK, KV_HEADS, HEAD)
        live = jnp.repeat((slot_ids < count).astype(jnp.float32), TILE_TOK)
        query_rows = query_block.astype(jnp.float32).reshape(TEXT, KV_HEADS, QUERY_HEADS, HEAD)
        query_norm = rms_scale(query_rows, query_gain).astype(jnp.bfloat16)
        scores = jnp.einsum('tvgh,kvh->vgtk', query_norm.astype(jnp.float32), key_list.astype(jnp.float32)) / math.sqrt(HEAD)
        weights = jnp.exp(scores) * live[None, None, None, :]
        totals = lax.optimization_barrier(jnp.sum(weights, axis=-1))
        accum = jnp.einsum('vgtk,kvh->tvgh', weights.astype(jnp.bfloat16).astype(jnp.float32), value_list.astype(jnp.float32))
        mixed = accum / jnp.transpose(totals, (2, 0, 1))[:, :, :, None] * gate_value[None, :, :, None]
        return mixed.reshape(TEXT, KV_HEADS * QUERY_HEADS * HEAD).astype(jnp.bfloat16)
    return lax.map(one_owner, (request_ids, queries))
```

```python
import functools
import math

import jax
import jax.numpy as jnp
from jax import lax
from jax.experimental import pallas as pl
from jax.experimental.pallas import tpu as pltpu
from jax.sharding import PartitionSpec as P

MAX_TILES = 4


EPS = 1e-05


def rms_scale(values, gain):
    mean_square = jnp.mean(values * values, axis=-1, keepdims=True)
    return values * lax.rsqrt(mean_square + EPS) * gain


def project_rows(states, w_key, w_value, key_gain, kv_heads):
    leading = states.shape[:-1]
    width = w_key.shape[1]
    head_size = width // kv_heads
    flat_rows = states.reshape(-1, states.shape[-1])
    key_sum = jnp.dot(
        flat_rows,
        lax.all_gather(w_key, "dec", axis=0, tiled=True),
        preferred_element_type=jnp.float32,
    )
    value_sum = jnp.dot(
        flat_rows,
        lax.all_gather(w_value, "dec", axis=0, tiled=True),
        preferred_element_type=jnp.float32,
    )
    key_heads = key_sum.reshape(-1, kv_heads, head_size)
    key_rows = rms_scale(key_heads, key_gain).astype(jnp.bfloat16).reshape(leading + (width,))
    value_rows = value_sum.astype(jnp.bfloat16).reshape(leading + (width,))
    return (key_rows, value_rows)


def attend_kernel(scale, head_size, q_ref, k_ref, v_ref, qgain_ref, gate_ref, live_ref, o_ref):
    slots = live_ref.shape[0]
    keys = k_ref.shape[0] // slots
    group_size = q_ref.shape[1] // head_size
    ones = jnp.ones((keys, head_size), jnp.bfloat16)
    gain = qgain_ref[...]
    blocks = []
    for j in range(slots):
        rows = pl.ds(j * keys, keys)
        blocks.append((k_ref[rows, :], jnp.concatenate([v_ref[rows, :], ones], axis=1)))
    for g in range(group_size):
        cols = pl.ds(g * head_size, head_size)
        q = q_ref[:, cols].astype(jnp.float32)
        q = rms_scale(q, gain).astype(jnp.bfloat16)
        acc = None
        for j in range(slots):
            key_block, value_block = blocks[j]
            scores = lax.dot_general(
                q, key_block, (((1,), (1,)), ((), ())), preferred_element_type=jnp.float32
            )
            weights = jnp.exp2(scores * scale).astype(jnp.bfloat16)
            part = jnp.dot(weights, value_block, preferred_element_type=jnp.float32)
            part = part * live_ref[j]
            acc = part if acc is None else acc + part
        gate = gate_ref[:, cols]
        o_ref[:, cols] = (acc[:, :head_size] / acc[:, head_size:] * gate).astype(o_ref.dtype)


def attend(queries, keys, values, query_gain, gates, live, head_size):
    text_len, width = queries.shape
    total = keys.shape[0]
    kv_heads = keys.shape[1] // head_size
    part = width // kv_heads
    scale = math.log2(math.e) / math.sqrt(head_size)
    return pl.pallas_call(
        functools.partial(attend_kernel, scale, head_size),
        grid=(kv_heads,),
        out_shape=jax.ShapeDtypeStruct((text_len, width), jnp.bfloat16),
        in_specs=[
            pl.BlockSpec((text_len, part), lambda h: (0, h)),
            pl.BlockSpec((total, head_size), lambda h: (0, h)),
            pl.BlockSpec((total, head_size), lambda h: (0, h)),
            pl.BlockSpec((1, head_size), lambda h: (0, 0)),
            pl.BlockSpec((1, part), lambda h: (0, h)),
            pl.BlockSpec(memory_space=pltpu.SMEM),
        ],
        out_specs=pl.BlockSpec((text_len, part), lambda h: (0, h)),
        compiler_params=pltpu.CompilerParams(vmem_limit_bytes=32 << 20),
    )(queries, keys, values, query_gain, gates, live)


def body(
    image_states, w_key, w_value, key_gain, query_gain, head_gate, queries, tile_counts, owner_of
):
    own_index = lax.axis_index("dec")
    tiles_total = image_states.shape[0]
    head_size = key_gain.shape[0]
    kv_heads = w_key.shape[1] // head_size
    request_ids = jnp.arange(owner_of.shape[0], dtype=jnp.int32)
    owned = owner_of[None, :] == request_ids[:, None]
    tile_starts = jnp.cumsum(tile_counts) - tile_counts
    peer_counts = jnp.sum(jnp.where(owned, tile_counts[None, :], 0), axis=1)
    peer_starts = jnp.sum(jnp.where(owned, tile_starts[None, :], 0), axis=1)
    slot_ids = jnp.arange(MAX_TILES, dtype=jnp.int32)
    wanted = jnp.minimum(peer_starts[None, :] + slot_ids[:, None], tiles_total - 1)
    in_use = slot_ids[:, None] < peer_counts[None, :]

    def pack(source):
        picked = jnp.take(source, wanted, axis=0)
        return jnp.where(in_use[:, :, None, None], picked, jnp.zeros((), source.dtype))

    own_count = jnp.sum(jnp.where(request_ids == own_index, peer_counts, 0))
    key_rows, value_rows = project_rows(image_states, w_key, w_value, key_gain, kv_heads)
    outgoing = (pack(key_rows), pack(value_rows))
    received = (
        lax.all_to_all(outgoing[0], "dec", split_axis=1, concat_axis=1, tiled=True),
        lax.all_to_all(outgoing[1], "dec", split_axis=1, concat_axis=1, tiled=True),
    )
    slot_live = (slot_ids < own_count).astype(jnp.float32)
    gates = jnp.repeat(jnp.tanh(head_gate), head_size)[None, :]
    width = kv_heads * head_size
    mixed = attend(
        queries[0],
        received[0].reshape(-1, width),
        received[1].reshape(-1, width),
        query_gain[None, :],
        gates,
        slot_live,
        head_size,
    )
    return mixed[None]


def solution(mesh):
    placed = (
        P("group", "dec", None),
        P("dec", None),
        P("dec", None),
        P(),
        P(),
        P(),
        P(("group", "dec"), None, None),
        P("group"),
        P("group"),
    )
    return jax.shard_map(
        body, mesh=mesh, in_specs=placed, out_specs=P(("group", "dec"), None, None), check_vma=False
    )
```

```python
import functools
import math

import jax
import jax.numpy as jnp
from jax import lax
from jax.experimental import pallas as pl
from jax.experimental.pallas import tpu as pltpu
from jax.sharding import PartitionSpec as P

MAX_TILES = 4


EPS = 1e-05


def rms_scale(values, gain):
    mean_square = jnp.mean(values * values, axis=-1, keepdims=True)
    return values * lax.rsqrt(mean_square + EPS) * gain


def project_rows(states, w_key, w_value, key_gain, kv_heads):
    leading = states.shape[:-1]
    width = w_key.shape[1]
    head_size = width // kv_heads
    flat_rows = states.reshape(-1, states.shape[-1])
    key_sum = jnp.dot(
        flat_rows,
        lax.all_gather(w_key, "dec", axis=0, tiled=True),
        preferred_element_type=jnp.float32,
    )
    value_sum = jnp.dot(
        flat_rows,
        lax.all_gather(w_value, "dec", axis=0, tiled=True),
        preferred_element_type=jnp.float32,
    )
    key_heads = key_sum.reshape(-1, kv_heads, head_size)
    key_rows = rms_scale(key_heads, key_gain).astype(jnp.bfloat16).reshape(leading + (width,))
    value_rows = value_sum.astype(jnp.bfloat16).reshape(leading + (width,))
    return (key_rows, value_rows)


def attend_kernel(scale, head_size, q_ref, k_ref, v_ref, qgain_ref, gate_ref, live_ref, o_ref):
    slots = live_ref.shape[0]
    keys = k_ref.shape[0] // slots
    group_size = q_ref.shape[1] // head_size
    ones = jnp.ones((keys, head_size), jnp.bfloat16)
    gain = qgain_ref[...]
    blocks = []
    for j in range(slots):
        rows = pl.ds(j * keys, keys)
        blocks.append((k_ref[rows, :], jnp.concatenate([v_ref[rows, :], ones], axis=1)))
    for g in range(group_size):
        cols = pl.ds(g * head_size, head_size)
        q = q_ref[:, cols].astype(jnp.float32)
        q = rms_scale(q, gain).astype(jnp.bfloat16)
        acc = None
        for j in range(slots):
            key_block, value_block = blocks[j]
            scores = lax.dot_general(
                q, key_block, (((1,), (1,)), ((), ())), preferred_element_type=jnp.float32
            )
            weights = jnp.exp2(scores * scale).astype(jnp.bfloat16)
            part = jnp.dot(weights, value_block, preferred_element_type=jnp.float32)
            part = part * live_ref[j]
            acc = part if acc is None else acc + part
        gate = gate_ref[:, cols]
        o_ref[:, cols] = (acc[:, :head_size] / acc[:, head_size:] * gate).astype(o_ref.dtype)


def attend(queries, routed, query_gain, gates, live, head_size):
    text_len, width = queries.shape
    total = routed.shape[1]
    kv_heads = routed.shape[2] // head_size
    part = width // kv_heads
    scale = math.log2(math.e) / math.sqrt(head_size)
    return pl.pallas_call(
        functools.partial(attend_kernel, scale, head_size),
        grid=(kv_heads,),
        out_shape=jax.ShapeDtypeStruct((text_len, width), jnp.bfloat16),
        in_specs=[
            pl.BlockSpec((text_len, part), lambda h: (0, h)),
            pl.BlockSpec((None, total, head_size), lambda h: (0, 0, h)),
            pl.BlockSpec((None, total, head_size), lambda h: (1, 0, h)),
            pl.BlockSpec((1, head_size), lambda h: (0, 0)),
            pl.BlockSpec((1, part), lambda h: (0, h)),
            pl.BlockSpec(memory_space=pltpu.SMEM),
        ],
        out_specs=pl.BlockSpec((text_len, part), lambda h: (0, h)),
        compiler_params=pltpu.CompilerParams(vmem_limit_bytes=32 << 20),
    )(queries, routed, routed, query_gain, gates, live)


PIECES = 8
Z_PIECES = 6
X_PIECES = 5
Z_SIZE = 4


def route_kernel(
    head_size,
    x_hbm,
    wk_hbm,
    wv_hbm,
    kgain_ref,
    wanted_ref,
    out_ref,
    x_buf,
    w_buf,
    acc,
    kv_buf,
    pack,
    load_sem,
    z_recv,
    x_recv,
    ya_recv,
    yb_recv,
    sib_recv,
    zup_send,
    zdn_send,
    x_send,
    ya_send,
    yb_send,
    sib_send,
    a2a_send,
    a2a_recv,
    own_sem,
):
    me = lax.axis_index("dec")
    y = lax.axis_index("group")
    devices = pack.shape[1]
    slots = pack.shape[0]
    z, x, c = me // 4, (me // 2) % 2, me % 2
    rows, depth, width = w_buf.shape[1], w_buf.shape[1] * PIECES // 2, w_buf.shape[2]
    sib = {"dec": me + 1 - 2 * c}
    x_peer = {"dec": me + 2 - 4 * x}
    y_peer = {"group": 1 - y}
    up = {"dec": lax.rem(me + 4, devices)}
    down = {"dec": lax.rem(me + devices - 4, devices)}

    half = PIECES // 2
    loads = [
        pltpu.make_async_copy(x_hbm, x_buf, load_sem.at[0]),
    ]
    for i in range(half):
        part = pl.ds(i * rows, rows)
        loads.append(
            pltpu.make_async_copy(
                wk_hbm.at[part, :], w_buf.at[me * PIECES + i], load_sem.at[1 + i]
            )
        )
        loads.append(
            pltpu.make_async_copy(
                wv_hbm.at[part, :], w_buf.at[me * PIECES + half + i], load_sem.at[1 + half + i]
            )
        )
    for load in loads[1:]:
        load.start()
    loads[0].start()

    barrier = pltpu.get_barrier_semaphore()

    @pl.loop(1, devices)
    def _(i):
        pl.semaphore_signal(
            barrier,
            inc=1,
            device_id={"dec": lax.rem(me + i, devices)},
            device_id_type=pl.DeviceIdType.MESH,
        )

    pl.semaphore_signal(barrier, inc=1, device_id=y_peer, device_id_type=pl.DeviceIdType.MESH)
    pl.semaphore_wait(barrier, devices)

    def shard_of(zs, xs, cs):
        return (zs * 2 + xs) * 2 + cs

    def move(first, count, send_sem, recv_sem, peer):
        part = w_buf.at[pl.ds(first, count)]
        return pltpu.make_async_remote_copy(
            src_ref=part,
            dst_ref=part,
            send_sem=send_sem,
            recv_sem=recv_sem,
            device_id=peer,
            device_id_type=pl.DeviceIdType.MESH,
        )

    def piece(q):
        return q + y * (PIECES - 1 - 2 * q)

    def near(zs):
        return zs * 2 + x

    def far(zs):
        return zs * 2 + 1 - x

    def to_up(zs, q):
        return move(
            shard_of(zs, x, c) * PIECES + piece(q), 1, zup_send.at[zs], z_recv.at[zs, q], up
        )

    def to_down(zs, q):
        return move(
            shard_of(zs, x, c) * PIECES + piece(q), 1, zdn_send.at[zs], z_recv.at[zs, q], down
        )

    def to_x(zs, q):
        return move(
            shard_of(zs, x, c) * PIECES + piece(q), 1, x_send.at[zs], x_recv.at[zs, q], x_peer
        )

    def to_sib(zs, xs, first, count):
        index = zs * 2 + xs
        return move(
            shard_of(zs, xs, c) * PIECES + first, count, sib_send.at[index], sib_recv.at[index], sib
        )

    for load in loads[1:]:
        load.wait()

    @pl.loop(0, PIECES)
    def _(q):
        @pl.when(q < Z_PIECES)
        def _():
            @pl.when(z < Z_SIZE - 1)
            def _():
                to_up(z, q).start()

            @pl.when(z > 0)
            def _():
                to_down(z, q).start()

        @pl.when(q < X_PIECES)
        def _():
            to_x(z, q).start()

    to_sib(z, x, 0, PIECES).start()
    acc[...] = jnp.zeros_like(acc)
    loads[0].wait()

    def in_line(step, low, d):
        zs = z + (2 * d - 1) * step
        ok = (step >= low) & (step < Z_SIZE) & (zs >= 0) & (zs < Z_SIZE)
        return zs, ok & ((d == 0) | (step > 0))

    a_late = PIECES - Z_PIECES
    b_late = PIECES - X_PIECES

    @pl.loop(0, Z_SIZE + 2)
    def _(t):
        for d in range(2):
            zs, ok = in_line(t - 1, 1, d)

            @pl.when(ok)
            def _():
                first = Z_PIECES * (1 - y)
                base = shard_of(zs, x, c) * PIECES
                move(base + first, a_late, ya_send.at[zs], ya_recv.at[zs], y_peer).wait_recv()
                to_sib(zs, x, first, a_late).start()

            zb, okb = in_line(t - 2, 0, d)

            @pl.when(okb)
            def _():
                first = X_PIECES * (1 - y)
                base = shard_of(zb, 1 - x, c) * PIECES
                move(base + first, b_late, yb_send.at[zb], yb_recv.at[zb], y_peer).wait_recv()
                to_sib(zb, 1 - x, first, b_late).start()

        @pl.loop(0, PIECES)
        def _(q):
            for d in range(2):
                zs, ok = in_line(t, 1, d)

                @pl.when(ok & (q < Z_PIECES))
                def _():
                    if d == 0:
                        to_up(zs, q).wait_recv()

                        @pl.when(z < Z_SIZE - 1)
                        def _():
                            to_up(zs, q).start()
                    else:
                        to_down(zs, q).wait_recv()

                        @pl.when(z > 0)
                        def _():
                            to_down(zs, q).start()

                    @pl.when(q < X_PIECES)
                    def _():
                        to_x(zs, q).start()

                    @pl.when(q < a_late)
                    def _():
                        move(
                            shard_of(zs, x, c) * PIECES + piece(q),
                            1,
                            ya_send.at[zs],
                            ya_recv.at[zs],
                            y_peer,
                        ).start()

                    to_sib(zs, x, piece(q), 1).start()

                zb, okb = in_line(t - 1, 0, d)

                @pl.when(okb & (q < X_PIECES))
                def _():
                    first = shard_of(zb, 1 - x, c) * PIECES + piece(q)
                    move(first, 1, x_send.at[zb], x_recv.at[zb, q], x_peer).wait_recv()

                    @pl.when(q < b_late)
                    def _():
                        move(first, 1, yb_send.at[zb], yb_recv.at[zb], y_peer).start()

                    to_sib(zb, 1 - x, piece(q), 1).start()

            other = q // 4
            is_far = (q // 2) % 2
            d = q % 2
            zm, okm = in_line(t - 1 - is_far, 0, d)

            @pl.when(okm)
            def _():
                xm = x + is_far * (1 - 2 * x)
                cm = c + other * (1 - 2 * c)

                @pl.when(other == 1)
                def _():
                    index = zm * 2 + xm
                    move(
                        shard_of(zm, xm, cm) * PIECES,
                        PIECES,
                        sib_send.at[index],
                        sib_recv.at[index],
                        sib,
                    ).wait_recv()

                shard = shard_of(zm, xm, cm)
                cols = pl.ds(pl.multiple_of(shard * depth, depth), depth)
                for k in range(2):
                    block = w_buf[pl.ds(shard * PIECES + k * half, half)].reshape(depth, width)
                    out = pl.ds(k * width, width)
                    acc[:, out] += jnp.dot(
                        x_buf[:, cols], block, preferred_element_type=jnp.float32
                    )

    tiles = kv_buf.shape[0]
    tokens = kv_buf.shape[2]
    for h in range(width // head_size):
        cols = pl.ds(h * head_size, head_size)
        keys = rms_scale(acc[:, cols], kgain_ref[...]).astype(jnp.bfloat16)
        kv_buf[:, 0, :, cols] = keys.reshape(tiles, tokens, head_size)
    kv_buf[:, 1, :, :] = acc[:, width:].astype(jnp.bfloat16).reshape(tiles, tokens, width)

    def exchange(j, dest):
        return pltpu.make_async_remote_copy(
            src_ref=pack.at[j, dest],
            dst_ref=out_ref.at[:, j, me],
            send_sem=a2a_send.at[j],
            recv_sem=a2a_recv.at[j],
            device_id={"dec": dest},
            device_id_type=pl.DeviceIdType.MESH,
        )

    @pl.loop(0, slots)
    def _(j):
        @pl.loop(1, devices)
        def _(i):
            dest = lax.rem(me + i, devices)
            pack[j, dest] = kv_buf[wanted_ref[j, dest]]
            exchange(j, dest).start()

        pack[j, me] = kv_buf[wanted_ref[j, me]]
        pltpu.make_async_copy(pack.at[j, me], out_ref.at[:, j, me], own_sem.at[j]).start()

    for zs in range(Z_SIZE):

        @pl.when((z >= zs) & (z < Z_SIZE - 1))
        def _():
            move(zs * PIECES, Z_PIECES, zup_send.at[zs], z_recv.at[zs, 0], up).wait_send()

        @pl.when((z <= zs) & (z > 0))
        def _():
            move(zs * PIECES, Z_PIECES, zdn_send.at[zs], z_recv.at[zs, 0], down).wait_send()

        move(zs * PIECES, X_PIECES, x_send.at[zs], x_recv.at[zs, 0], x_peer).wait_send()

        @pl.when(z != zs)
        def _():
            move(zs * PIECES, a_late, ya_send.at[zs], ya_recv.at[zs], y_peer).wait_send()

        move(zs * PIECES, b_late, yb_send.at[zs], yb_recv.at[zs], y_peer).wait_send()
        for xs in range(2):
            to_sib(zs, xs, 0, PIECES).wait_send()

    for j in range(slots):
        pltpu.make_async_copy(pack.at[j, me], out_ref.at[:, j, me], own_sem.at[j]).wait()
        whole = pltpu.make_async_remote_copy(
            src_ref=pack.at[j, pl.ds(0, devices - 1)],
            dst_ref=pack.at[j, pl.ds(0, devices - 1)],
            send_sem=a2a_send.at[j],
            recv_sem=a2a_recv.at[j],
            device_id=sib,
            device_id_type=pl.DeviceIdType.MESH,
        )
        whole.wait_send()
        whole.wait_recv()


def project_and_route(states, w_key, w_value, key_gain, wanted):
    tiles, tokens, model = states.shape
    slots, devices = wanted.shape
    depth, width = w_key.shape
    head_size = key_gain.shape[0]
    flat = tiles * tokens
    shards = devices // 2
    dma = pltpu.SemaphoreType.DMA
    return pl.pallas_call(
        functools.partial(route_kernel, head_size),
        out_shape=jax.ShapeDtypeStruct((2, slots, devices, tokens, width), jnp.bfloat16),
        in_specs=[
            pl.BlockSpec(memory_space=pl.ANY),
            pl.BlockSpec(memory_space=pl.ANY),
            pl.BlockSpec(memory_space=pl.ANY),
            pl.BlockSpec(memory_space=pltpu.VMEM),
            pl.BlockSpec(memory_space=pltpu.SMEM),
        ],
        out_specs=pl.BlockSpec(memory_space=pl.ANY),
        scratch_shapes=[
            pltpu.VMEM((flat, model), jnp.bfloat16),
            pltpu.VMEM((devices * PIECES, 2 * depth // PIECES, width), jnp.bfloat16),
            pltpu.VMEM((flat, 2 * width), jnp.float32),
            pltpu.VMEM((tiles, 2, tokens, width), jnp.bfloat16),
            pltpu.VMEM((slots, devices, 2, tokens, width), jnp.bfloat16),
            dma((1 + PIECES,)),
            dma((Z_SIZE, Z_PIECES)),
            dma((Z_SIZE, X_PIECES)),
            dma((Z_SIZE,)),
            dma((Z_SIZE,)),
            dma((shards,)),
            dma((Z_SIZE,)),
            dma((Z_SIZE,)),
            dma((Z_SIZE,)),
            dma((Z_SIZE,)),
            dma((Z_SIZE,)),
            dma((shards,)),
            dma((slots,)),
            dma((slots,)),
            dma((slots,)),
        ],
        compiler_params=pltpu.CompilerParams(
            collective_id=0, has_side_effects=True, vmem_limit_bytes=48 << 20
        ),
        cost_estimate=pl.CostEstimate(
            flops=4 * flat * model * width, bytes_accessed=40 << 20, transcendentals=0
        ),
    )(states.reshape(flat, model), w_key, w_value, key_gain[None, :], wanted)


def body(
    on_grid, image_states, w_key, w_value, key_gain, query_gain, head_gate, queries, tile_counts, owner_of
):
    own_index = lax.axis_index("dec")
    tiles_total = image_states.shape[0]
    head_size = key_gain.shape[0]
    kv_heads = w_key.shape[1] // head_size
    request_ids = jnp.arange(owner_of.shape[0], dtype=jnp.int32)
    owned = owner_of[None, :] == request_ids[:, None]
    tile_starts = jnp.cumsum(tile_counts) - tile_counts
    peer_counts = jnp.sum(jnp.where(owned, tile_counts[None, :], 0), axis=1)
    peer_starts = jnp.sum(jnp.where(owned, tile_starts[None, :], 0), axis=1)
    slot_ids = jnp.arange(MAX_TILES, dtype=jnp.int32)
    wanted = jnp.minimum(peer_starts[None, :] + slot_ids[:, None], tiles_total - 1)

    def pack(source):
        return jnp.take(source, wanted, axis=0)

    own_count = jnp.sum(jnp.where(request_ids == own_index, peer_counts, 0))
    width = kv_heads * head_size
    if on_grid:
        routed = project_and_route(image_states, w_key, w_value, key_gain, wanted)
        routed = routed.reshape(2, -1, width)
    else:
        rows = project_rows(image_states, w_key, w_value, key_gain, kv_heads)
        routed = jnp.stack(
            [
                lax.all_to_all(pack(part), "dec", split_axis=1, concat_axis=1, tiled=True)
                for part in rows
            ]
        ).reshape(2, -1, width)
    slot_live = (slot_ids < own_count).astype(jnp.float32)
    gates = jnp.repeat(jnp.tanh(head_gate), head_size)[None, :]
    mixed = attend(queries[0], routed, query_gain[None, :], gates, slot_live, head_size)
    return mixed[None]


def solution(mesh):
    placed = (
        P("group", "dec", None),
        P("dec", None),
        P("dec", None),
        P(),
        P(),
        P(),
        P(("group", "dec"), None, None),
        P("group"),
        P("group"),
    )
    on_grid = mesh.shape["dec"] == 16 and mesh.shape["group"] == 2
    return jax.shard_map(
        functools.partial(body, on_grid), mesh=mesh, in_specs=placed, out_specs=P(("group", "dec"), None, None), check_vma=False
    )
```

```python
import functools
import math

import jax
import jax.numpy as jnp
from jax import lax
from jax.experimental import pallas as pl
from jax.experimental.pallas import tpu as pltpu
from jax.sharding import PartitionSpec as P

MAX_TILES = 4


EPS = 1e-05


def rms_scale(values, gain):
    mean_square = jnp.mean(values * values, axis=-1, keepdims=True)
    return values * lax.rsqrt(mean_square + EPS) * gain


def project_rows(states, w_key, w_value, key_gain, kv_heads):
    leading = states.shape[:-1]
    width = w_key.shape[1]
    head_size = width // kv_heads
    flat_rows = states.reshape(-1, states.shape[-1])
    key_sum = jnp.dot(
        flat_rows,
        lax.all_gather(w_key, "dec", axis=0, tiled=True),
        preferred_element_type=jnp.float32,
    )
    value_sum = jnp.dot(
        flat_rows,
        lax.all_gather(w_value, "dec", axis=0, tiled=True),
        preferred_element_type=jnp.float32,
    )
    key_heads = key_sum.reshape(-1, kv_heads, head_size)
    key_rows = rms_scale(key_heads, key_gain).astype(jnp.bfloat16).reshape(leading + (width,))
    value_rows = value_sum.astype(jnp.bfloat16).reshape(leading + (width,))
    return (key_rows, value_rows)


def attend_kernel(scale, head_size, q_ref, k_ref, v_ref, qgain_ref, gate_ref, live_ref, o_ref):
    slots = live_ref.shape[0]
    keys = k_ref.shape[0] // slots
    group_size = q_ref.shape[1] // head_size
    ones = jnp.ones((keys, head_size), jnp.bfloat16)
    gain = qgain_ref[...]
    blocks = []
    for j in range(slots):
        rows = pl.ds(j * keys, keys)
        blocks.append((k_ref[rows, :], jnp.concatenate([v_ref[rows, :], ones], axis=1)))
    for g in range(group_size):
        cols = pl.ds(g * head_size, head_size)
        q = q_ref[:, cols].astype(jnp.float32)
        q = rms_scale(q, gain).astype(jnp.bfloat16)
        acc = None
        for j in range(slots):
            key_block, value_block = blocks[j]
            scores = lax.dot_general(
                q, key_block, (((1,), (1,)), ((), ())), preferred_element_type=jnp.float32
            )
            weights = jnp.exp2(scores * scale).astype(jnp.bfloat16)
            part = jnp.dot(weights, value_block, preferred_element_type=jnp.float32)
            part = part * live_ref[j]
            acc = part if acc is None else acc + part
        gate = gate_ref[:, cols]
        o_ref[:, cols] = (acc[:, :head_size] / acc[:, head_size:] * gate).astype(o_ref.dtype)


def attend(queries, routed, query_gain, gates, live, head_size):
    text_len, width = queries.shape
    total = routed.shape[1]
    kv_heads = routed.shape[2] // head_size
    part = width // kv_heads
    scale = math.log2(math.e) / math.sqrt(head_size)
    return pl.pallas_call(
        functools.partial(attend_kernel, scale, head_size),
        grid=(kv_heads,),
        out_shape=jax.ShapeDtypeStruct((text_len, width), jnp.bfloat16),
        in_specs=[
            pl.BlockSpec((text_len, part), lambda h: (0, h)),
            pl.BlockSpec((None, total, head_size), lambda h: (0, 0, h)),
            pl.BlockSpec((None, total, head_size), lambda h: (1, 0, h)),
            pl.BlockSpec((1, head_size), lambda h: (0, 0)),
            pl.BlockSpec((1, part), lambda h: (0, h)),
            pl.BlockSpec(memory_space=pltpu.SMEM),
        ],
        out_specs=pl.BlockSpec((text_len, part), lambda h: (0, h)),
        compiler_params=pltpu.CompilerParams(vmem_limit_bytes=32 << 20),
    )(queries, routed, routed, query_gain, gates, live)


PIECES = 8
Z_PIECES = 6
X_PIECES = 5
Z_SIZE = 4


def route_kernel(
    head_size,
    x_hbm,
    wk_hbm,
    wv_hbm,
    kgain_ref,
    qgain_ref,
    gate_ref,
    q_hbm,
    wanted_ref,
    live_ref,
    out_ref,
    x_buf,
    w_buf,
    acc,
    kv_buf,
    pack,
    recv0,
    recv1,
    recv2,
    recv3,
    q_raw,
    q_buf,
    mix,
    gates,
    small_sem,
    load_sem,
    z_recv,
    x_recv,
    ya_recv,
    yb_recv,
    sib_recv,
    zup_send,
    zdn_send,
    x_send,
    ya_send,
    yb_send,
    sib_send,
    a2a_send,
    a2a_recv,
    own_sem,
):
    recv = (recv0, recv1, recv2, recv3)
    me = lax.axis_index("dec")
    y = lax.axis_index("group")
    devices = pack.shape[1]
    slots = pack.shape[0]
    z, x, c = me // 4, (me // 2) % 2, me % 2
    rows, depth, width = w_buf.shape[1], w_buf.shape[1] * PIECES // 2, w_buf.shape[2]
    sib = {"dec": me + 1 - 2 * c}
    x_peer = {"dec": me + 2 - 4 * x}
    y_peer = {"group": 1 - y}
    up = {"dec": lax.rem(me + 4, devices)}
    down = {"dec": lax.rem(me + devices - 4, devices)}

    half = PIECES // 2
    loads = [
        pltpu.make_async_copy(x_hbm, x_buf, load_sem.at[0]),
    ]
    for i in range(half):
        part = pl.ds(i * rows, rows)
        loads.append(
            pltpu.make_async_copy(
                wk_hbm.at[part, :], w_buf.at[me * PIECES + i], load_sem.at[1 + i]
            )
        )
        loads.append(
            pltpu.make_async_copy(
                wv_hbm.at[part, :], w_buf.at[me * PIECES + half + i], load_sem.at[1 + half + i]
            )
        )
    for load in loads[1:]:
        load.start()
    loads[0].start()
    staged = (
        (q_hbm, q_raw),
    )
    smalls = [
        pltpu.make_async_copy(source, target, small_sem.at[i])
        for i, (source, target) in enumerate(staged)
    ]
    for small in smalls:
        small.start()

    barrier = pltpu.get_barrier_semaphore()

    @pl.loop(1, devices)
    def _(i):
        pl.semaphore_signal(
            barrier,
            inc=1,
            device_id={"dec": lax.rem(me + i, devices)},
            device_id_type=pl.DeviceIdType.MESH,
        )

    pl.semaphore_signal(barrier, inc=1, device_id=y_peer, device_id_type=pl.DeviceIdType.MESH)
    pl.semaphore_wait(barrier, devices)

    def shard_of(zs, xs, cs):
        return (zs * 2 + xs) * 2 + cs

    def move(first, count, send_sem, recv_sem, peer):
        part = w_buf.at[pl.ds(first, count)]
        return pltpu.make_async_remote_copy(
            src_ref=part,
            dst_ref=part,
            send_sem=send_sem,
            recv_sem=recv_sem,
            device_id=peer,
            device_id_type=pl.DeviceIdType.MESH,
        )

    def piece(q):
        return q + y * (PIECES - 1 - 2 * q)

    def near(zs):
        return zs * 2 + x

    def far(zs):
        return zs * 2 + 1 - x

    def to_up(zs, q):
        return move(
            shard_of(zs, x, c) * PIECES + piece(q), 1, zup_send.at[zs], z_recv.at[zs, q], up
        )

    def to_down(zs, q):
        return move(
            shard_of(zs, x, c) * PIECES + piece(q), 1, zdn_send.at[zs], z_recv.at[zs, q], down
        )

    def to_x(zs, q):
        return move(
            shard_of(zs, x, c) * PIECES + piece(q), 1, x_send.at[zs], x_recv.at[zs, q], x_peer
        )

    def to_sib(zs, xs, first, count):
        index = zs * 2 + xs
        return move(
            shard_of(zs, xs, c) * PIECES + first, count, sib_send.at[index], sib_recv.at[index], sib
        )

    for load in loads[1:]:
        load.wait()

    @pl.loop(0, PIECES)
    def _(q):
        @pl.when(q < Z_PIECES)
        def _():
            @pl.when(z < Z_SIZE - 1)
            def _():
                to_up(z, q).start()

            @pl.when(z > 0)
            def _():
                to_down(z, q).start()

        @pl.when(q < X_PIECES)
        def _():
            to_x(z, q).start()

    to_sib(z, x, 0, PIECES).start()
    acc[...] = jnp.zeros_like(acc)
    for small in smalls:
        small.wait()
    loads[0].wait()

    def in_line(step, low, d):
        zs = z + (2 * d - 1) * step
        ok = (step >= low) & (step < Z_SIZE) & (zs >= 0) & (zs < Z_SIZE)
        return zs, ok & ((d == 0) | (step > 0))

    a_late = PIECES - Z_PIECES
    b_late = PIECES - X_PIECES

    @pl.loop(0, Z_SIZE + 2)
    def _(t):
        for d in range(2):
            zs, ok = in_line(t - 1, 1, d)

            @pl.when(ok)
            def _():
                first = Z_PIECES * (1 - y)
                base = shard_of(zs, x, c) * PIECES
                move(base + first, a_late, ya_send.at[zs], ya_recv.at[zs], y_peer).wait_recv()
                to_sib(zs, x, first, a_late).start()

            zb, okb = in_line(t - 2, 0, d)

            @pl.when(okb)
            def _():
                first = X_PIECES * (1 - y)
                base = shard_of(zb, 1 - x, c) * PIECES
                move(base + first, b_late, yb_send.at[zb], yb_recv.at[zb], y_peer).wait_recv()
                to_sib(zb, 1 - x, first, b_late).start()

        @pl.loop(0, PIECES)
        def _(q):
            for d in range(2):
                zs, ok = in_line(t, 1, d)

                @pl.when(ok & (q < Z_PIECES))
                def _():
                    if d == 0:
                        to_up(zs, q).wait_recv()

                        @pl.when(z < Z_SIZE - 1)
                        def _():
                            to_up(zs, q).start()
                    else:
                        to_down(zs, q).wait_recv()

                        @pl.when(z > 0)
                        def _():
                            to_down(zs, q).start()

                    @pl.when(q < X_PIECES)
                    def _():
                        to_x(zs, q).start()

                    @pl.when(q < a_late)
                    def _():
                        move(
                            shard_of(zs, x, c) * PIECES + piece(q),
                            1,
                            ya_send.at[zs],
                            ya_recv.at[zs],
                            y_peer,
                        ).start()

                    to_sib(zs, x, piece(q), 1).start()

                zb, okb = in_line(t - 1, 0, d)

                @pl.when(okb & (q < X_PIECES))
                def _():
                    first = shard_of(zb, 1 - x, c) * PIECES + piece(q)
                    move(first, 1, x_send.at[zb], x_recv.at[zb, q], x_peer).wait_recv()

                    @pl.when(q < b_late)
                    def _():
                        move(first, 1, yb_send.at[zb], yb_recv.at[zb], y_peer).start()

                    to_sib(zb, 1 - x, piece(q), 1).start()

            other = q // 4
            is_far = (q // 2) % 2
            d = q % 2
            zm, okm = in_line(t - 1 - is_far, 0, d)

            @pl.when(okm)
            def _():
                xm = x + is_far * (1 - 2 * x)
                cm = c + other * (1 - 2 * c)

                @pl.when(other == 1)
                def _():
                    index = zm * 2 + xm
                    move(
                        shard_of(zm, xm, cm) * PIECES,
                        PIECES,
                        sib_send.at[index],
                        sib_recv.at[index],
                        sib,
                    ).wait_recv()

                shard = shard_of(zm, xm, cm)
                cols = pl.ds(pl.multiple_of(shard * depth, depth), depth)
                for k in range(2):
                    block = w_buf[pl.ds(shard * PIECES + k * half, half)].reshape(depth, width)
                    out = pl.ds(k * width, width)
                    acc[:, out] += jnp.dot(
                        x_buf[:, cols], block, preferred_element_type=jnp.float32
                    )

    tiles = kv_buf.shape[0]
    tokens = kv_buf.shape[2]
    for h in range(width // head_size):
        cols = pl.ds(h * head_size, head_size)
        keys = rms_scale(acc[:, cols], kgain_ref[...]).astype(jnp.bfloat16)
        kv_buf[:, 0, :, cols] = keys.reshape(tiles, tokens, head_size)
    kv_buf[:, 1, :, :] = acc[:, width:].astype(jnp.bfloat16).reshape(tiles, tokens, width)

    def exchange(j, dest):
        return pltpu.make_async_remote_copy(
            src_ref=pack.at[j, dest],
            dst_ref=recv[j].at[me],
            send_sem=a2a_send.at[j],
            recv_sem=a2a_recv.at[j, me],
            device_id={"dec": dest},
            device_id_type=pl.DeviceIdType.MESH,
        )

    for j in range(slots):

        @pl.loop(1, devices)
        def _(i):
            dest = lax.rem(me + i, devices)
            pack[j, dest] = kv_buf[wanted_ref[j, dest]]
            exchange(j, dest).start()

        pack[j, me] = kv_buf[wanted_ref[j, me]]
        pltpu.make_async_copy(pack.at[j, me], recv[j].at[me], own_sem.at[j]).start()

    kv_heads = width // head_size
    heads = gates.shape[0]
    group_size = heads // kv_heads
    span = group_size * head_size
    keys_per_slot = devices * tokens
    scale = math.log2(math.e) / math.sqrt(head_size)
    gate_row = jnp.tanh(gate_ref[...])
    for k in range(heads):
        gates[k] = jnp.broadcast_to(gate_row[:, k : k + 1], gates.shape[1:])

    @pl.loop(0, heads)
    def _(k):
        cols = pl.ds(pl.multiple_of(k * head_size, head_size), head_size)
        q = rms_scale(q_raw[:, cols].astype(jnp.float32), qgain_ref[...])
        q_buf[:, cols] = q.astype(jnp.bfloat16)
        mix[k] = jnp.zeros(mix.shape[1:], mix.dtype)

    for zs in range(Z_SIZE):

        @pl.when((z >= zs) & (z < Z_SIZE - 1))
        def _():
            move(zs * PIECES, Z_PIECES, zup_send.at[zs], z_recv.at[zs, 0], up).wait_send()

        @pl.when((z <= zs) & (z > 0))
        def _():
            move(zs * PIECES, Z_PIECES, zdn_send.at[zs], z_recv.at[zs, 0], down).wait_send()

        move(zs * PIECES, X_PIECES, x_send.at[zs], x_recv.at[zs, 0], x_peer).wait_send()

        @pl.when(z != zs)
        def _():
            move(zs * PIECES, a_late, ya_send.at[zs], ya_recv.at[zs], y_peer).wait_send()

        move(zs * PIECES, b_late, yb_send.at[zs], yb_recv.at[zs], y_peer).wait_send()
        for xs in range(2):
            to_sib(zs, xs, 0, PIECES).wait_send()

    def arrived(j):
        pltpu.make_async_copy(pack.at[j, me], recv[j].at[me], own_sem.at[j]).wait()

        @pl.loop(1, devices)
        def _(i):
            source = lax.rem(me + i, devices)
            pltpu.make_async_remote_copy(
                src_ref=pack.at[j, source],
                dst_ref=recv[j].at[source],
                send_sem=a2a_send.at[j],
                recv_sem=a2a_recv.at[j, source],
                device_id={"dec": source},
                device_id_type=pl.DeviceIdType.MESH,
            ).wait_recv()

    def attend_slot(j, last):
        arrived(j)
        live = live_ref[j]
        ones = jnp.ones((keys_per_slot, head_size), jnp.bfloat16)

        @pl.loop(0, kv_heads)
        def _(h):
            head = pl.ds(pl.multiple_of(h * head_size, head_size), head_size)
            keys = recv[j][:, 0, :, head].reshape(keys_per_slot, head_size)
            values = recv[j][:, 1, :, head].reshape(keys_per_slot, head_size)
            values = jnp.concatenate([values, ones], axis=1)
            for g in range(group_size):
                k = h * group_size + g
                cols = pl.ds(pl.multiple_of(k * head_size, head_size), head_size)
                scores = lax.dot_general(
                    q_buf[:, cols],
                    keys,
                    (((1,), (1,)), ((), ())),
                    preferred_element_type=jnp.float32,
                )
                weights = jnp.exp2(scores * scale).astype(jnp.bfloat16)
                part = jnp.dot(weights, values, preferred_element_type=jnp.float32)
                part = mix[k] + part * live
                if last:
                    ratio = part[:, :head_size] / part[:, head_size:] * gates[k][:1]
                    out_ref[:, cols] = ratio.astype(out_ref.dtype)
                else:
                    mix[k] = part

    for j in range(slots):
        attend_slot(j, j == slots - 1)
    for j in range(slots):
        pltpu.make_async_remote_copy(
            src_ref=pack.at[j, pl.ds(0, devices - 1)],
            dst_ref=recv[j].at[pl.ds(0, devices - 1)],
            send_sem=a2a_send.at[j],
            recv_sem=a2a_recv.at[j, 0],
            device_id=sib,
            device_id_type=pl.DeviceIdType.MESH,
        ).wait_send()


def attend_on_grid(
    states, w_key, w_value, key_gain, query_gain, head_gate, queries, wanted, live
):
    tiles, tokens, model = states.shape
    slots, devices = wanted.shape
    depth, width = w_key.shape
    text_len, model_out = queries.shape
    heads = head_gate.shape[0]
    head_size = key_gain.shape[0]
    flat = tiles * tokens
    shards = devices // 2
    dma = pltpu.SemaphoreType.DMA
    return pl.pallas_call(
        functools.partial(route_kernel, head_size),
        out_shape=jax.ShapeDtypeStruct((text_len, model_out), jnp.bfloat16),
        in_specs=[pl.BlockSpec(memory_space=pl.ANY)] * 3
        + [pl.BlockSpec(memory_space=pltpu.VMEM)] * 3
        + [pl.BlockSpec(memory_space=pl.ANY)]
        + [pl.BlockSpec(memory_space=pltpu.SMEM)] * 2,
        out_specs=pl.BlockSpec(memory_space=pltpu.VMEM),
        scratch_shapes=[
            pltpu.VMEM((flat, model), jnp.bfloat16),
            pltpu.VMEM((devices * PIECES, 2 * depth // PIECES, width), jnp.bfloat16),
            pltpu.VMEM((flat, 2 * width), jnp.float32),
            pltpu.VMEM((tiles, 2, tokens, width), jnp.bfloat16),
            pltpu.VMEM((slots, devices, 2, tokens, width), jnp.bfloat16),
            pltpu.VMEM((devices, 2, tokens, width), jnp.bfloat16),
            pltpu.VMEM((devices, 2, tokens, width), jnp.bfloat16),
            pltpu.VMEM((devices, 2, tokens, width), jnp.bfloat16),
            pltpu.VMEM((devices, 2, tokens, width), jnp.bfloat16),
            pltpu.VMEM((text_len, model_out), jnp.bfloat16),
            pltpu.VMEM((text_len, model_out), jnp.bfloat16),
            pltpu.VMEM((heads, text_len, 2 * head_size), jnp.float32),
            pltpu.VMEM((heads, 8, head_size), jnp.float32),
            dma((1,)),
            dma((1 + PIECES,)),
            dma((Z_SIZE, Z_PIECES)),
            dma((Z_SIZE, X_PIECES)),
            dma((Z_SIZE,)),
            dma((Z_SIZE,)),
            dma((shards,)),
            dma((Z_SIZE,)),
            dma((Z_SIZE,)),
            dma((Z_SIZE,)),
            dma((Z_SIZE,)),
            dma((Z_SIZE,)),
            dma((shards,)),
            dma((slots,)),
            dma((slots, devices)),
            dma((slots,)),
        ],
        compiler_params=pltpu.CompilerParams(
            collective_id=0, has_side_effects=True, vmem_limit_bytes=56 << 20
        ),
        cost_estimate=pl.CostEstimate(
            flops=4 * flat * model * width, bytes_accessed=40 << 20, transcendentals=0
        ),
    )(
        states.reshape(flat, model),
        w_key,
        w_value,
        key_gain[None, :],
        query_gain[None, :],
        head_gate[None, :],
        queries,
        wanted,
        live,
    )


def body(
    on_grid, image_states, w_key, w_value, key_gain, query_gain, head_gate, queries, tile_counts, owner_of
):
    own_index = lax.axis_index("dec")
    tiles_total = image_states.shape[0]
    head_size = key_gain.shape[0]
    kv_heads = w_key.shape[1] // head_size
    request_ids = jnp.arange(owner_of.shape[0], dtype=jnp.int32)
    owned = owner_of[None, :] == request_ids[:, None]
    tile_starts = jnp.cumsum(tile_counts) - tile_counts
    peer_counts = jnp.sum(jnp.where(owned, tile_counts[None, :], 0), axis=1)
    peer_starts = jnp.sum(jnp.where(owned, tile_starts[None, :], 0), axis=1)
    slot_ids = jnp.arange(MAX_TILES, dtype=jnp.int32)
    wanted = jnp.minimum(peer_starts[None, :] + slot_ids[:, None], tiles_total - 1)

    def pack(source):
        return jnp.take(source, wanted, axis=0)

    own_count = jnp.sum(jnp.where(request_ids == own_index, peer_counts, 0))
    slot_live = (slot_ids < own_count).astype(jnp.float32)
    if on_grid:
        return attend_on_grid(
            image_states,
            w_key,
            w_value,
            key_gain,
            query_gain,
            head_gate,
            queries[0],
            wanted,
            slot_live,
        )[None]
    width = kv_heads * head_size
    rows = project_rows(image_states, w_key, w_value, key_gain, kv_heads)
    routed = jnp.stack(
        [
            lax.all_to_all(pack(part), "dec", split_axis=1, concat_axis=1, tiled=True)
            for part in rows
        ]
    ).reshape(2, -1, width)
    gates = jnp.repeat(jnp.tanh(head_gate), head_size)[None, :]
    mixed = attend(queries[0], routed, query_gain[None, :], gates, slot_live, head_size)
    return mixed[None]


def solution(mesh):
    placed = (
        P("group", "dec", None),
        P("dec", None),
        P("dec", None),
        P(),
        P(),
        P(),
        P(("group", "dec"), None, None),
        P("group"),
        P("group"),
    )
    on_grid = mesh.shape["dec"] == 16 and mesh.shape["group"] == 2
    return jax.shard_map(
        functools.partial(body, on_grid), mesh=mesh, in_specs=placed, out_specs=P(("group", "dec"), None, None), check_vma=False
    )
```
